32 devices in a mesh: ctx: 4 (over y, core), tp: 4 (over z), rep: 2 (over x).
Axes of the slice: x: 2, y: 2, z: 4, core: 2. Of those that a mesh axis runs over, the one named last changes fastest.
Arguments:
- queries: bfloat16 [1536, 4096], P(('ctx', 'rep'), 'tp'), may hold values from -6 to 6
- key_states: bfloat16 [1536, 1024], P(('ctx', 'rep'), 'tp'), may hold values from -6 to 6
- value_states: bfloat16 [1536, 1024], P(('ctx', 'rep'), 'tp'), may hold values from -6 to 6
- out_grad: bfloat16 [1536, 4096], P(('ctx', 'rep'), 'tp'), may hold values from -6 to 6
- doc_lengths: int32 [7], replicated, may hold values from 0 to 768, as said below
Outputs:
- attended: bfloat16 [1536, 4096], P(('ctx', 'rep'), 'tp')
- query_grad: bfloat16 [1536, 4096], P(('ctx', 'rep'), 'tp')
- key_grad: bfloat16 [1536, 1024], P(('ctx', 'rep'), 'tp')
- value_grad: bfloat16 [1536, 1024], P(('ctx', 'rep'), 'tp')
The draws below stay inside these ranges and needn't reach their ends.
Inputs may be any that keep to these rules, and one draw needn't show every extreme that they name: `doc_lengths`: the lengths sum to 1536; the largest is exactly 768; some entries are 0.
All inputs are finite; a program needn't handle non-finite values.
Results may differ from the reference program's by a relative error of at most 0.007.
Values may be sent and summed in bfloat16 or wider, within the bound.
A program may use at most 64 MiB of HBM per device.

```python
import math
import jax
import jax.numpy as jnp
from jax import lax

HQ = 32
HK = 8
HD = 128
TOK_DEV = 192
REACH = 4
TOKENS = 1536
MOST = 768


def layout(key):
    folded = jax.random.fold_in(key, 11)
    key_offset, key_cuts, key_whole, key_forced = jax.random.split(folded, 4)
    group_count = TOKENS // MOST - 1
    offset = jax.random.randint(key_offset, (), 1, TOK_DEV)
    cut_points = jnp.sort(jax.random.randint(key_cuts, (group_count, 3), 0, MOST - 1), axis=1)
    whole_flag = jax.random.randint(key_whole, (group_count, 1), 0, 2)
    forced = jax.random.randint(key_forced, (), 0, group_count)
    forced_flag = (jnp.arange(group_count) == forced).astype(jnp.int32)[:, None]
    whole_flag = jnp.maximum(whole_flag, forced_flag)
    cut_points = cut_points * (1 - whole_flag)
    return (offset, cut_points)


def draw_doc_lengths(key, part):
    offset, cut_points = layout(key)
    group_count = cut_points.shape[0]
    edges = jnp.concatenate([jnp.zeros((group_count, 1), jnp.int32), cut_points.astype(jnp.int32), jnp.full((group_count, 1), MOST, jnp.int32)], axis=1)
    pieces = (edges[:, 1:] - edges[:, :-1]).reshape(-1)
    rest_len = TOKENS - offset - group_count * MOST
    first_half = rest_len // 2
    tail_pair = jnp.stack([first_half, rest_len - first_half]).astype(jnp.int32)
    return jnp.concatenate([offset.astype(jnp.int32)[None], pieces, tail_pair]).astype(jnp.int32)


def draw_queries(key, part):
    drawn = jnp.clip(jax.random.normal(jax.random.fold_in(key, 21), (TOKENS, HQ * HD), jnp.float32), -4.0, 4.0)
    return drawn.astype(jnp.bfloat16)


def draw_key_states(key, part):
    drawn = jnp.clip(jax.random.normal(jax.random.fold_in(key, 22), (TOKENS, HK * HD), jnp.float32), -4.0, 4.0)
    return drawn.astype(jnp.bfloat16)


def block_scale(rng, dims, cuts, least, largest):
    factor_of = 1.0
    for dim, parts in cuts:
        steps = jax.random.uniform(jax.random.fold_in(jax.random.fold_in(rng, 6), dim), (parts,), jnp.float32, least / len(cuts), largest / len(cuts))
        factor_of = factor_of * jnp.repeat(jnp.exp(steps), dims[dim] // parts).reshape((-1,) + (1,) * (len(dims) - 1 - dim))
    return factor_of


def centred(stream_key, dims, width, bound, cuts=(), kind=jnp.bfloat16):
    values = jax.random.normal(stream_key, dims, jnp.float32) * width
    if len(cuts) > 0:
        values = block_scale(stream_key, dims, cuts, -0.22, 0.18) * values
    return jnp.clip(values, min=-bound, max=bound).astype(kind)


def setup_inputs(seed: int = 0) -> dict:
    keys = jax.random.split(jax.random.key(seed), 6)
    queries = draw_queries(jax.random.fold_in(keys[5], 71), 0)
    key_states = draw_key_states(jax.random.fold_in(keys[5], 71), 0)
    value_states = centred(keys[2], (TOKENS, HK * HD), 1.0, 6.0, ((0, 8), (1, 4)))
    out_grad = centred(keys[3], (TOKENS, HQ * HD), 1.0, 6.0, ((0, 8), (1, 4)))
    doc_lengths = draw_doc_lengths(jax.random.fold_in(keys[5], 71), 0)
    return dict(queries=queries, key_states=key_states, value_states=value_states, out_grad=out_grad, doc_lengths=doc_lengths)


masked_score = -1e+30

def document_of(doc_ends, positions):
    return lax.optimization_barrier(jnp.sum((doc_ends[None, :] <= positions[:, None]).astype(jnp.int32), axis=1))

def reference(queries, key_states, value_states, out_grad, doc_lengths):
    doc_ends = jnp.cumsum(doc_lengths).astype(jnp.int32)
    kv_heads = key_states.shape[1] // HD
    query_width = queries.shape[1]
    group_size = query_width // HD // kv_heads
    key_width = key_states.shape[1]
    scaling = 1.0 / math.sqrt(HD)
    block_count = TOKENS // TOK_DEV
    window = (REACH + 1) * TOK_DEV
    padding = jnp.zeros((REACH * TOK_DEV, key_width), key_states.dtype)
    key_padded = jnp.concatenate([padding, key_states], axis=0)
    value_padded = jnp.concatenate([padding, value_states], axis=0)
    query_tail = jnp.zeros((REACH * TOK_DEV, query_width), queries.dtype)
    query_padded = jnp.concatenate([queries, query_tail], axis=0)
    grad_padded = jnp.concatenate([out_grad, query_tail.astype(out_grad.dtype)], axis=0)
    highest = lax.Precision.HIGHEST

    def forward_block(block_index):
        start = (block_index * TOK_DEV).astype(jnp.int32)
        query_block = lax.dynamic_slice_in_dim(queries, start, TOK_DEV, 0).astype(jnp.float32)
        query_block = query_block.reshape(TOK_DEV, kv_heads, group_size, HD)
        grad_block = lax.dynamic_slice_in_dim(out_grad, start, TOK_DEV, 0).astype(jnp.float32)
        grad_block = grad_block.reshape(TOK_DEV, kv_heads, group_size, HD)
        key_window = lax.dynamic_slice_in_dim(key_padded, start, window, 0).astype(jnp.float32)
        key_window = key_window.reshape(window, kv_heads, HD)
        value_window = lax.dynamic_slice_in_dim(value_padded, start, window, 0).astype(jnp.float32)
        value_window = value_window.reshape(window, kv_heads, HD)
        query_pos = start + jnp.arange(TOK_DEV, dtype=jnp.int32)
        key_pos = start - REACH * TOK_DEV + jnp.arange(window, dtype=jnp.int32)
        allowed = document_of(doc_ends, key_pos)[None, :] == document_of(doc_ends, query_pos)[:, None]
        allowed = allowed & (key_pos[None, :] <= query_pos[:, None]) & (key_pos[None, :] >= 0)
        scores = jnp.einsum('tgjd,sgd->gjts', query_block, key_window, precision=highest) * scaling
        scores = jnp.where(allowed[None, None], scores, masked_score)
        row_max = lax.optimization_barrier(jnp.max(scores, axis=-1, keepdims=True))
        log_total = row_max + jnp.log(lax.optimization_barrier(jnp.sum(jnp.exp(scores - row_max), axis=-1, keepdims=True)))
        probs = jnp.exp(scores - log_total)
        probs_bf = lax.optimization_barrier(probs.astype(jnp.bfloat16)).astype(jnp.float32)
        attended = jnp.einsum('gjts,sgd->tgjd', probs_bf, value_window, precision=highest)
        attended_bf = lax.optimization_barrier(attended.astype(jnp.bfloat16))
        delta_row = lax.optimization_barrier(jnp.sum(grad_block * attended_bf.astype(jnp.float32), axis=-1))
        dprobs = jnp.einsum('tgjd,sgd->gjts', grad_block, value_window, precision=highest)
        dscores = probs * (dprobs - jnp.transpose(delta_row, (1, 2, 0))[..., None])
        dscores = lax.optimization_barrier(dscores.astype(jnp.bfloat16)).astype(jnp.float32)
        query_grad = jnp.einsum('gjts,sgd->tgjd', dscores, key_window, precision=highest) * scaling
        return (attended_bf.reshape(TOK_DEV, query_width), query_grad.astype(jnp.bfloat16).reshape(TOK_DEV, query_width), log_total[..., 0], delta_row)
    attended_stack, query_stack, log_stack, delta_stack = lax.map(forward_block, jnp.arange(block_count, dtype=jnp.int32))
    log_padded = jnp.concatenate([log_stack, jnp.zeros((REACH, kv_heads, group_size, TOK_DEV), jnp.float32)], axis=0)
    delta_flat = delta_stack.reshape(TOKENS, kv_heads, group_size)
    delta_padded = jnp.concatenate([delta_flat, jnp.zeros((REACH * TOK_DEV, kv_heads, group_size), jnp.float32)], axis=0)

    def backward_keys(block_index):
        start = (block_index * TOK_DEV).astype(jnp.int32)
        key_block = lax.dynamic_slice_in_dim(key_states, start, TOK_DEV, 0).astype(jnp.float32)
        key_block = key_block.reshape(TOK_DEV, kv_heads, HD)
        value_block = lax.dynamic_slice_in_dim(value_states, start, TOK_DEV, 0).astype(jnp.float32)
        value_block = value_block.reshape(TOK_DEV, kv_heads, HD)
        query_window = lax.dynamic_slice_in_dim(query_padded, start, window, 0).astype(jnp.float32)
        query_window = query_window.reshape(window, kv_heads, group_size, HD)
        grad_window = lax.dynamic_slice_in_dim(grad_padded, start, window, 0).astype(jnp.float32)
        grad_window = grad_window.reshape(window, kv_heads, group_size, HD)
        log_window = lax.dynamic_slice_in_dim(log_padded, block_index, REACH + 1, 0)
        log_window = jnp.transpose(log_window, (1, 2, 0, 3)).reshape(kv_heads, group_size, window)
        delta_window = lax.dynamic_slice_in_dim(delta_padded, start, window, 0)
        delta_window = jnp.transpose(delta_window, (1, 2, 0))
        query_pos = start + jnp.arange(window, dtype=jnp.int32)
        key_pos = start + jnp.arange(TOK_DEV, dtype=jnp.int32)
        allowed = document_of(doc_ends, query_pos)[:, None] == document_of(doc_ends, key_pos)[None, :]
        allowed = allowed & (key_pos[None, :] <= query_pos[:, None]) & (query_pos[:, None] < TOKENS)
        scores = jnp.einsum('tgjd,sgd->gjts', query_window, key_block, precision=highest) * scaling
        scores = jnp.where(allowed[None, None], scores, masked_score)
        probs = jnp.exp(scores - log_window[..., None])
        probs_bf = lax.optimization_barrier(probs.astype(jnp.bfloat16)).astype(jnp.float32)
        dprobs = jnp.einsum('tgjd,sgd->gjts', grad_window, value_block, precision=highest)
        dscores = probs * (dprobs - delta_window[..., None])
        dscores = lax.optimization_barrier(dscores.astype(jnp.bfloat16)).astype(jnp.float32)
        key_grad = jnp.einsum('gjts,tgjd->sgd', dscores, query_window, precision=highest) * scaling
        value_grad = jnp.einsum('gjts,tgjd->sgd', probs_bf, grad_window, precision=highest)
        return (key_grad.astype(jnp.bfloat16).reshape(TOK_DEV, key_width), value_grad.astype(jnp.bfloat16).reshape(TOK_DEV, key_width))
    key_stack, value_stack = lax.map(backward_keys, jnp.arange(block_count, dtype=jnp.int32))
    attended_all = attended_stack.reshape(TOKENS, query_width)
    query_all = query_stack.reshape(TOKENS, query_width)
    key_all = key_stack.reshape(TOKENS, key_width)
    value_all = value_stack.reshape(TOKENS, key_width)
    return (attended_all, query_all, key_all, value_all)
```

```python
import functools
import math

import jax
import jax.numpy as jnp
from jax import lax
from jax.experimental import pallas as pl
from jax.experimental.pallas import tpu as pltpu
from jax.sharding import PartitionSpec as P

HD = 128
REACH = 4
MESH = pl.DeviceIdType.MESH
masked_score = -1e30


def dot(a, b):
    return jnp.dot(a, b, preferred_element_type=jnp.float32)


def kernel(
    n, reps, doc_ref, q_ref, k_ref, v_ref, do_ref, att_ref, dq_ref, dk_ref, dv_ref,
    kv, gout, gin, scores, probs, kv_send, kv_recv, g_send, g_recv,
):
    rows = q_ref.shape[0]
    kv_heads = k_ref.shape[1] // HD
    group_size = q_ref.shape[1] // HD // kv_heads
    width = group_size * rows
    scaling = 1.0 / math.sqrt(HD)
    log2e = math.log2(math.e)
    pos = lax.axis_index("ctx") * reps + lax.axis_index("rep")

    def place(p):
        return {"ctx": p // reps, "rep": lax.rem(p, reps)}

    barrier = pltpu.get_barrier_semaphore()
    for d in range(1, REACH + 1):
        for ok, peer in ((pos + d < n, pos + d), (pos >= d, pos - d)):

            @pl.when(ok)
            def _():
                pl.semaphore_signal(barrier, inc=1, device_id=place(peer), device_id_type=MESH)

    for g in range(kv_heads):
        cols = slice(g * HD, (g + 1) * HD)
        kv[g, 0, :, :HD] = k_ref[:, cols]
        kv[g, 0, :, HD:] = v_ref[:, cols]
    pl.semaphore_wait(barrier, jnp.minimum(pos, REACH) + jnp.minimum(n - 1 - pos, REACH))

    def kv_copy(g, d):
        return pltpu.make_async_remote_copy(
            src_ref=kv.at[g, 0], dst_ref=kv.at[g, d], send_sem=kv_send.at[g, d - 1],
            recv_sem=kv_recv.at[g, d - 1], device_id=place(pos + d), device_id_type=MESH,
        )

    def g_copy(g, d):
        return pltpu.make_async_remote_copy(
            src_ref=gout.at[g, d - 1], dst_ref=gin.at[g, d - 1], send_sem=g_send.at[g, d - 1],
            recv_sem=g_recv.at[g, d - 1], device_id=place(pos - d), device_id_type=MESH,
        )

    for g in range(kv_heads):
        for d in range(1, REACH + 1):

            @pl.when(pos + d < n)
            def _():
                kv_copy(g, d).start()

    for d in range(1, REACH + 1):

        @pl.when(pos < d)
        def _():
            for g in range(kv_heads):
                kv[g, d] = jnp.zeros(kv.shape[2:], kv.dtype)

        @pl.when(pos + d >= n)
        def _():
            for g in range(kv_heads):
                gin[g, d - 1] = jnp.zeros(gin.shape[2:], gin.dtype)

    first = pos * rows
    query_pos = first + lax.rem(lax.broadcasted_iota(jnp.int32, (1, width), 1), rows)
    begin = jnp.zeros((1, width), jnp.int32)
    end = jnp.int32(0)
    for i in range(doc_ref.shape[0]):
        end = end + doc_ref[i]
        begin = jnp.maximum(begin, jnp.where(query_pos >= end, end, 0))

    own_grads = []
    for g in range(kv_heads):
        heads = [g * group_size + j for j in range(group_size)]
        q = jnp.concatenate([q_ref[:, h * HD : (h + 1) * HD] for h in heads], axis=0)
        do = jnp.concatenate([do_ref[:, h * HD : (h + 1) * HD] for h in heads], axis=0)
        q_t = q.T
        do_t = do.T

        top = None
        for d in range(REACH + 1):
            if d:

                @pl.when(pos >= d)
                def _():
                    kv_copy(g, d).wait_recv()

            key_pos = first - d * rows + lax.broadcasted_iota(jnp.int32, (rows, 1), 0)
            allowed = key_pos >= begin
            if d == 0:
                allowed = allowed & (key_pos <= query_pos)
            s = jnp.where(allowed, dot(kv[g, d, :, :HD], q_t) * (scaling * log2e), masked_score)
            scores[d] = s
            most = jnp.max(s, axis=0, keepdims=True)
            top = most if top is None else jnp.maximum(top, most)
        total = jnp.zeros((1, width), jnp.float32)
        for d in range(REACH + 1):
            e = jnp.exp2(scores[d] - top)
            scores[d] = e
            total = total + jnp.sum(e, axis=0, keepdims=True)
        inverse = 1.0 / total
        att_t = jnp.zeros((HD, width), jnp.float32)
        for d in range(REACH + 1):
            p_bf = (scores[d] * inverse).astype(jnp.bfloat16)
            probs[d] = p_bf
            att_t = att_t + dot(kv[g, d, :, HD:].T, p_bf)
        att_bf = att_t.astype(jnp.bfloat16)
        delta = jnp.sum(
            att_bf.astype(jnp.float32) * do_t.astype(jnp.float32), axis=0, keepdims=True
        )
        dq_t = jnp.zeros((HD, width), jnp.float32)
        for d in range(REACH, -1, -1):
            dp = dot(kv[g, d, :, HD:], do_t)
            ds = (scores[d] * inverse * (dp - delta)).astype(jnp.bfloat16)
            dk = dot(ds, q) * scaling
            dv = dot(probs[d], do)
            dq_t = dq_t + dot(kv[g, d, :, :HD].T, ds)
            if d:
                gout[g, d - 1, :, :HD] = dk.astype(jnp.bfloat16)
                gout[g, d - 1, :, HD:] = dv.astype(jnp.bfloat16)

                @pl.when(pos >= d)
                def _():
                    g_copy(g, d).start()

            else:
                own_grads.append((dk, dv))
        att = att_t.T.astype(jnp.bfloat16)
        dq = (dq_t * scaling).T.astype(jnp.bfloat16)
        for j, h in enumerate(heads):
            att_ref[:, h * HD : (h + 1) * HD] = att[j * rows : (j + 1) * rows]
            dq_ref[:, h * HD : (h + 1) * HD] = dq[j * rows : (j + 1) * rows]

    for g in range(kv_heads):
        dk, dv = own_grads[g]
        for d in range(REACH, 0, -1):

            @pl.when(pos + d < n)
            def _():
                g_copy(g, d).wait_recv()

            dk = dk + gin[g, d - 1, :, :HD].astype(jnp.float32)
            dv = dv + gin[g, d - 1, :, HD:].astype(jnp.float32)
        dk_ref[:, g * HD : (g + 1) * HD] = dk.astype(jnp.bfloat16)
        dv_ref[:, g * HD : (g + 1) * HD] = dv.astype(jnp.bfloat16)
    for g in range(kv_heads):
        for d in range(1, REACH + 1):

            @pl.when(pos + d < n)
            def _():
                kv_copy(g, d).wait_send()

            @pl.when(pos >= d)
            def _():
                g_copy(g, d).wait_send()


def per_device(n, reps, queries, key_states, value_states, out_grad, doc_lengths):
    rows, key_width = key_states.shape
    kv_heads = key_width // HD
    width = rows * (queries.shape[1] // key_width)
    vmem = pl.BlockSpec(memory_space=pltpu.VMEM)
    like = [jax.ShapeDtypeStruct(x.shape, x.dtype) for x in (queries, queries, key_states, key_states)]
    sems = pltpu.SemaphoreType.DMA((kv_heads, REACH))
    return tuple(
        pl.pallas_call(
            functools.partial(kernel, n, reps),
            out_shape=like,
            in_specs=[pl.BlockSpec(memory_space=pltpu.SMEM)] + [vmem] * 4,
            out_specs=[vmem] * 4,
            scratch_shapes=[
                pltpu.VMEM((kv_heads, REACH + 1, rows, 2 * HD), jnp.bfloat16),
                pltpu.VMEM((kv_heads, REACH, rows, 2 * HD), jnp.bfloat16),
                pltpu.VMEM((kv_heads, REACH, rows, 2 * HD), jnp.bfloat16),
                pltpu.VMEM((REACH + 1, rows, width), jnp.float32),
                pltpu.VMEM((REACH + 1, rows, width), jnp.bfloat16),
                sems, sems, sems, sems,
            ],
            compiler_params=pltpu.CompilerParams(
                collective_id=0, has_side_effects=True, vmem_limit_bytes=40 * 1024 * 1024
            ),
        )(doc_lengths, queries, key_states, value_states, out_grad)
    )


def solution(mesh):
    split = P(("ctx", "rep"), "tp")
    reps = mesh.shape["rep"]
    return jax.shard_map(
        functools.partial(per_device, mesh.shape["ctx"] * reps, reps),
        mesh=mesh,
        in_specs=(split, split, split, split, P()),
        out_specs=(split, split, split, split),
        check_vma=False,
    )
```

```python
import functools
import math

import jax
import jax.numpy as jnp
from jax import lax
from jax.experimental import pallas as pl
from jax.experimental.pallas import tpu as pltpu
from jax.sharding import PartitionSpec as P

HD = 128
REACH = 4
MESH = pl.DeviceIdType.MESH
masked_score = -1e30


def dot(a, b):
    return jnp.dot(a, b, preferred_element_type=jnp.float32)


def kernel(
    n, reps, doc_hbm, q_hbm, k_ref, v_ref, do_hbm, att_hbm, dq_hbm, dk_hbm, dv_hbm,
    att_ref, dq_ref, dk_ref, dv_ref, store, doc_ref, q_ref, do_ref, kv, gout, gin, scores, probs, load, kv_send, kv_recv, g_send, g_recv,
):
    rows = q_ref.shape[0]
    kv_heads = k_ref.shape[1] // HD
    group_size = q_ref.shape[1] // HD // kv_heads
    width = group_size * rows
    scaling = 1.0 / math.sqrt(HD)
    log2e = math.log2(math.e)
    pos = lax.axis_index("ctx") * reps + lax.axis_index("rep")

    def place(p):
        return {"ctx": p // reps, "rep": lax.rem(p, reps)}

    barrier = pltpu.get_barrier_semaphore()
    for d in range(1, REACH + 1):
        for ok, peer in ((pos + d < n, pos + d), (pos >= d, pos - d)):

            @pl.when(ok)
            def _():
                pl.semaphore_signal(barrier, inc=1, device_id=place(peer), device_id_type=MESH)

    kv_loads = []
    for g in range(kv_heads):
        cols = pl.ds(g * HD, HD)
        for i, ref in enumerate((k_ref, v_ref)):
            kv_loads.append(
                pltpu.make_async_copy(
                    ref.at[:, cols], kv.at[g, 0, :, pl.ds(i * HD, HD)], load.at[3 + 2 * g + i]
                )
            )
    loads = [
        pltpu.make_async_copy(doc_hbm, doc_ref, load.at[0]),
        pltpu.make_async_copy(q_hbm, q_ref, load.at[1]),
        pltpu.make_async_copy(do_hbm, do_ref, load.at[2]),
    ]
    for copy in kv_loads + loads:
        copy.start()
    for copy in kv_loads:
        copy.wait()
    pl.semaphore_wait(barrier, jnp.minimum(pos, REACH) + jnp.minimum(n - 1 - pos, REACH))

    def kv_copy(g, d):
        return pltpu.make_async_remote_copy(
            src_ref=kv.at[g, 0], dst_ref=kv.at[g, d], send_sem=kv_send.at[g, d - 1],
            recv_sem=kv_recv.at[g, d - 1], device_id=place(pos + d), device_id_type=MESH,
        )

    def g_copy(g, d):
        return pltpu.make_async_remote_copy(
            src_ref=gout.at[g, d - 1], dst_ref=gin.at[g, d - 1], send_sem=g_send.at[g, d - 1],
            recv_sem=g_recv.at[g, d - 1], device_id=place(pos - d), device_id_type=MESH,
        )

    for g in range(kv_heads):
        for d in range(1, REACH + 1):

            @pl.when(pos + d < n)
            def _():
                kv_copy(g, d).start()

    for d in range(1, REACH + 1):

        @pl.when(pos < d)
        def _():
            for g in range(kv_heads):
                kv[g, d] = jnp.zeros(kv.shape[2:], kv.dtype)

        @pl.when(pos + d >= n)
        def _():
            for g in range(kv_heads):
                gin[g, d - 1] = jnp.zeros(gin.shape[2:], gin.dtype)

    for copy in loads:
        copy.wait()
    first = pos * rows
    query_pos = first + lax.rem(lax.broadcasted_iota(jnp.int32, (1, width), 1), rows)
    begin = jnp.zeros((1, width), jnp.int32)
    end = jnp.int32(0)
    for i in range(doc_ref.shape[0]):
        end = end + doc_ref[i]
        begin = jnp.maximum(begin, jnp.where(query_pos >= end, end, 0))

    stores = []

    def store_columns(g, i, buf, out):
        cols = pl.ds(g * (buf.shape[1] // kv_heads), buf.shape[1] // kv_heads)
        copy = pltpu.make_async_copy(buf.at[:, cols], out.at[:, cols], store.at[g, i])
        copy.start()
        stores.append(copy)

    own_grads = []
    for g in range(kv_heads):
        heads = [g * group_size + j for j in range(group_size)]
        q = jnp.concatenate([q_ref[:, h * HD : (h + 1) * HD] for h in heads], axis=0)
        do = jnp.concatenate([do_ref[:, h * HD : (h + 1) * HD] for h in heads], axis=0)
        q_t = q.T
        do_t = do.T

        top = None
        for d in range(REACH + 1):
            if d:

                @pl.when(pos >= d)
                def _():
                    kv_copy(g, d).wait_recv()

            key_pos = first - d * rows + lax.broadcasted_iota(jnp.int32, (rows, 1), 0)
            allowed = key_pos >= begin
            if d == 0:
                allowed = allowed & (key_pos <= query_pos)
            s = jnp.where(allowed, dot(kv[g, d, :, :HD], q_t) * (scaling * log2e), masked_score)
            scores[d] = s
            most = jnp.max(s, axis=0, keepdims=True)
            top = most if top is None else jnp.maximum(top, most)
        total = jnp.zeros((1, width), jnp.float32)
        for d in range(REACH + 1):
            e = jnp.exp2(scores[d] - top)
            scores[d] = e
            total = total + jnp.sum(e, axis=0, keepdims=True)
        inverse = 1.0 / total
        att_t = jnp.zeros((HD, width), jnp.float32)
        for d in range(REACH + 1):
            p_bf = (scores[d] * inverse).astype(jnp.bfloat16)
            probs[d] = p_bf
            att_t = att_t + dot(kv[g, d, :, HD:].T, p_bf)
        att_bf = att_t.astype(jnp.bfloat16)
        delta = jnp.sum(
            att_bf.astype(jnp.float32) * do_t.astype(jnp.float32), axis=0, keepdims=True
        )
        dq_t = jnp.zeros((HD, width), jnp.float32)
        for d in range(REACH, -1, -1):
            dp = dot(kv[g, d, :, HD:], do_t)
            ds = (scores[d] * inverse * (dp - delta)).astype(jnp.bfloat16)
            dk = dot(ds, q) * scaling
            dv = dot(probs[d], do)
            dq_t = dq_t + dot(kv[g, d, :, :HD].T, ds)
            if d:
                gout[g, d - 1, :, :HD] = dk.astype(jnp.bfloat16)
                gout[g, d - 1, :, HD:] = dv.astype(jnp.bfloat16)

                @pl.when(pos >= d)
                def _():
                    g_copy(g, d).start()

            else:
                own_grads.append((dk, dv))
        att = att_t.T.astype(jnp.bfloat16)
        dq = (dq_t * scaling).T.astype(jnp.bfloat16)
        for j, h in enumerate(heads):
            att_ref[:, h * HD : (h + 1) * HD] = att[j * rows : (j + 1) * rows]
            dq_ref[:, h * HD : (h + 1) * HD] = dq[j * rows : (j + 1) * rows]
        store_columns(g, 0, att_ref, att_hbm)
        store_columns(g, 1, dq_ref, dq_hbm)

    for g in range(kv_heads):
        dk, dv = own_grads[g]
        for d in range(REACH, 0, -1):

            @pl.when(pos + d < n)
            def _():
                g_copy(g, d).wait_recv()

            dk = dk + gin[g, d - 1, :, :HD].astype(jnp.float32)
            dv = dv + gin[g, d - 1, :, HD:].astype(jnp.float32)
        dk_ref[:, g * HD : (g + 1) * HD] = dk.astype(jnp.bfloat16)
        dv_ref[:, g * HD : (g + 1) * HD] = dv.astype(jnp.bfloat16)
        store_columns(g, 2, dk_ref, dk_hbm)
        store_columns(g, 3, dv_ref, dv_hbm)
    for copy in stores:
        copy.wait()
    for g in range(kv_heads):
        for d in range(1, REACH + 1):

            @pl.when(pos + d < n)
            def _():
                kv_copy(g, d).wait_send()

            @pl.when(pos >= d)
            def _():
                g_copy(g, d).wait_send()


def flush(*refs):
    count = len(refs) // 2
    copies = [
        pltpu.make_async_copy(refs[i], refs[count + i], refs[-1].at[i]) for i in range(count)
    ]
    for copy in copies:
        copy.start()
    for copy in copies:
        copy.wait()


def per_device(n, reps, queries, key_states, value_states, out_grad, doc_lengths):
    rows, key_width = key_states.shape
    kv_heads = key_width // HD
    width = rows * (queries.shape[1] // key_width)
    like = [jax.ShapeDtypeStruct(x.shape, x.dtype) for x in (queries, queries, key_states, key_states)]
    sems = pltpu.SemaphoreType.DMA((kv_heads, REACH))
    hbm = pl.BlockSpec(memory_space=pltpu.HBM)
    results = pl.pallas_call(
        functools.partial(kernel, n, reps),
        out_shape=like,
        in_specs=[hbm] * 5,
        out_specs=[hbm] * 4,
        scratch_shapes=[
            *(pltpu.VMEM(x.shape, x.dtype) for x in like),
            pltpu.SemaphoreType.DMA((kv_heads, 4)),
            pltpu.SMEM(doc_lengths.shape, jnp.int32),
            pltpu.VMEM(queries.shape, queries.dtype),
            pltpu.VMEM(out_grad.shape, out_grad.dtype),
            pltpu.VMEM((kv_heads, REACH + 1, rows, 2 * HD), jnp.bfloat16),
            pltpu.VMEM((kv_heads, REACH, rows, 2 * HD), jnp.bfloat16),
            pltpu.VMEM((kv_heads, REACH, rows, 2 * HD), jnp.bfloat16),
            pltpu.VMEM((REACH + 1, rows, width), jnp.float32),
            pltpu.VMEM((REACH + 1, rows, width), jnp.bfloat16),
            pltpu.SemaphoreType.DMA((3 + 2 * kv_heads,)),
            sems, sems, sems, sems,
        ],
        compiler_params=pltpu.CompilerParams(
            collective_id=0, has_side_effects=True, vmem_limit_bytes=63 * 1024 * 1024
        ),
    )(doc_lengths, queries, key_states, value_states, out_grad)
    return tuple(
        pl.pallas_call(
            flush,
            out_shape=like,
            in_specs=[hbm] * 4,
            out_specs=[hbm] * 4,
            scratch_shapes=[pltpu.SemaphoreType.DMA((4,))],
        )(*results)
    )


def solution(mesh):
    split = P(("ctx", "rep"), "tp")
    reps = mesh.shape["rep"]
    return jax.shard_map(
        functools.partial(per_device, mesh.shape["ctx"] * reps, reps),
        mesh=mesh,
        in_specs=(split, split, split, split, P()),
        out_specs=(split, split, split, split),
        check_vma=False,
    )
```

```python
import functools
import math

import jax
import jax.numpy as jnp
from jax import lax
from jax.experimental import pallas as pl
from jax.experimental.pallas import tpu as pltpu
from jax.sharding import PartitionSpec as P

HD = 128
REACH = 4
MESH = pl.DeviceIdType.MESH
masked_score = -1e30


def dot(a, b):
    return jnp.dot(a, b, preferred_element_type=jnp.float32)


def kernel(
    n, reps, doc_hbm, q_hbm, k_ref, v_ref, do_hbm, att_hbm, dq_hbm, dk_hbm, dv_hbm,
    att_ref, dq_ref, dk_ref, dv_ref, store, doc_ref, q_ref, do_ref, kv, gout, gin, scores, probs, load, kv_send, kv_recv, g_send, g_recv,
):
    rows = q_ref.shape[0]
    kv_heads = k_ref.shape[1] // HD
    group_size = q_ref.shape[1] // HD // kv_heads
    width = group_size * rows
    scaling = 1.0 / math.sqrt(HD)
    log2e = math.log2(math.e)
    pos = lax.axis_index("ctx") * reps + lax.axis_index("rep")

    def place(p):
        return {"ctx": p // reps, "rep": lax.rem(p, reps)}

    barrier = pltpu.get_barrier_semaphore()
    for d in range(1, REACH + 1):
        for ok, peer in ((pos + d < n, pos + d), (pos >= d, pos - d)):

            @pl.when(ok)
            def _():
                pl.semaphore_signal(barrier, inc=1, device_id=place(peer), device_id_type=MESH)

    kv_loads = []
    for g in range(kv_heads):
        cols = pl.ds(g * HD, HD)
        for i, ref in enumerate((k_ref, v_ref)):
            kv_loads.append(
                pltpu.make_async_copy(
                    ref.at[:, cols], kv.at[g, 0, :, pl.ds(i * HD, HD)], load.at[3 + 2 * g + i]
                )
            )
    loads = [
        pltpu.make_async_copy(doc_hbm, doc_ref, load.at[0]),
        pltpu.make_async_copy(q_hbm, q_ref, load.at[1]),
        pltpu.make_async_copy(do_hbm, do_ref, load.at[2]),
    ]
    for copy in kv_loads + loads:
        copy.start()
    for copy in kv_loads:
        copy.wait()
    pl.semaphore_wait(barrier, jnp.minimum(pos, REACH) + jnp.minimum(n - 1 - pos, REACH))

    def kv_copy(g, d):
        return pltpu.make_async_remote_copy(
            src_ref=kv.at[g, 0], dst_ref=kv.at[g, d], send_sem=kv_send.at[g, d - 1],
            recv_sem=kv_recv.at[g, d - 1], device_id=place(pos + d), device_id_type=MESH,
        )

    def g_copy(g, d):
        return pltpu.make_async_remote_copy(
            src_ref=gout.at[g, d - 1], dst_ref=gin.at[g, d - 1], send_sem=g_send.at[g, d - 1],
            recv_sem=g_recv.at[g, d - 1], device_id=place(pos - d), device_id_type=MESH,
        )

    for g in range(kv_heads):
        for d in range(1, REACH + 1):

            @pl.when(pos + d < n)
            def _():
                kv_copy(g, d).start()

    for d in range(1, REACH + 1):

        @pl.when(pos < d)
        def _():
            for g in range(kv_heads):
                kv[g, d] = jnp.zeros(kv.shape[2:], kv.dtype)

        @pl.when(pos + d >= n)
        def _():
            for g in range(kv_heads):
                gin[g, d - 1] = jnp.zeros(gin.shape[2:], gin.dtype)

    for copy in loads:
        copy.wait()
    first = pos * rows
    query_pos = first + lax.rem(lax.broadcasted_iota(jnp.int32, (1, width), 1), rows)
    begin = jnp.zeros((1, width), jnp.int32)
    end = jnp.int32(0)
    for i in range(doc_ref.shape[0]):
        end = end + doc_ref[i]
        begin = jnp.maximum(begin, jnp.where(query_pos >= end, end, 0))

    stores = []

    def store_columns(g, i, buf, out):
        cols = pl.ds(g * (buf.shape[1] // kv_heads), buf.shape[1] // kv_heads)
        copy = pltpu.make_async_copy(buf.at[:, cols], out.at[:, cols], store.at[g, i])
        copy.start()
        stores.append(copy)

    own_grads = []
    for g in range(kv_heads):
        heads = [g * group_size + j for j in range(group_size)]
        q = jnp.concatenate([q_ref[:, h * HD : (h + 1) * HD] for h in heads], axis=0)
        do = jnp.concatenate([do_ref[:, h * HD : (h + 1) * HD] for h in heads], axis=0)
        q_t = q.T
        do_t = do.T

        top = None
        for d in range(REACH + 1):
            if d:

                @pl.when(pos >= d)
                def _():
                    kv_copy(g, d).wait_recv()

            key_pos = first - d * rows + lax.broadcasted_iota(jnp.int32, (rows, 1), 0)
            allowed = key_pos >= begin
            if d == 0:
                allowed = allowed & (key_pos <= query_pos)
            s = jnp.where(allowed, dot(kv[g, d, :, :HD], q_t) * (scaling * log2e), masked_score)
            scores[d] = s
            most = jnp.max(s, axis=0, keepdims=True)
            top = most if top is None else jnp.maximum(top, most)
        total = jnp.zeros((1, width), jnp.float32)
        for d in range(REACH + 1):
            e = jnp.exp2(scores[d] - top)
            scores[d] = e
            total = total + jnp.sum(e, axis=0, keepdims=True)
        inverse = 1.0 / total
        att_t = jnp.zeros((HD, width), jnp.float32)
        for d in range(REACH + 1):
            p_bf = (scores[d] * inverse).astype(jnp.bfloat16)
            probs[d] = p_bf
            att_t = att_t + dot(kv[g, d, :, HD:].T, p_bf)
        att_bf = att_t.astype(jnp.bfloat16)
        delta = jnp.sum(
            att_bf.astype(jnp.float32) * do_t.astype(jnp.float32), axis=0, keepdims=True
        )
        dq_t = jnp.zeros((HD, width), jnp.float32)
        for d in range(REACH, -1, -1):
            dp = dot(kv[g, d, :, HD:], do_t)
            ds = (scores[d] * inverse * (dp - delta)).astype(jnp.bfloat16)
            dk = dot(ds, q) * scaling
            dv = dot(probs[d], do)
            dq_t = dq_t + dot(kv[g, d, :, :HD].T, ds)
            if d:
                gout[g, d - 1, :, :HD] = dk.astype(jnp.bfloat16)
                gout[g, d - 1, :, HD:] = dv.astype(jnp.bfloat16)

                @pl.when(pos >= d)
                def _():
                    g_copy(g, d).start()

            else:
                own_grads.append((dk, dv))
        att = att_t.T.astype(jnp.bfloat16)
        dq = (dq_t * scaling).T.astype(jnp.bfloat16)
        for j, h in enumerate(heads):
            att_ref[:, h * HD : (h + 1) * HD] = att[j * rows : (j + 1) * rows]
            dq_ref[:, h * HD : (h + 1) * HD] = dq[j * rows : (j + 1) * rows]
        store_columns(g, 0, att_ref, att_hbm)
        store_columns(g, 1, dq_ref, dq_hbm)

    for g in range(kv_heads):
        dk, dv = own_grads[g]
        for d in range(REACH, 0, -1):

            @pl.when(pos + d < n)
            def _():
                g_copy(g, d).wait_recv()

            dk = dk + gin[g, d - 1, :, :HD].astype(jnp.float32)
            dv = dv + gin[g, d - 1, :, HD:].astype(jnp.float32)
        dk_ref[:, g * HD : (g + 1) * HD] = dk.astype(jnp.bfloat16)
        dv_ref[:, g * HD : (g + 1) * HD] = dv.astype(jnp.bfloat16)
        store_columns(g, 2, dk_ref, dk_hbm)
        store_columns(g, 3, dv_ref, dv_hbm)
    for copy in stores:
        copy.wait()
    for g in range(kv_heads):
        for d in range(1, REACH + 1):

            @pl.when(pos + d < n)
            def _():
                kv_copy(g, d).wait_send()

            @pl.when(pos >= d)
            def _():
                g_copy(g, d).wait_send()


def flush(*refs):
    count = 4
    ins, outs, bufs, sems = refs[:count], refs[count : 2 * count], refs[2 * count : -1], refs[-1]
    loads = [pltpu.make_async_copy(ins[i], bufs[i], sems.at[0, i]) for i in range(count)]
    stores = [pltpu.make_async_copy(bufs[i], outs[i], sems.at[1, i]) for i in range(count)]
    for copy in loads:
        copy.start()
    for load, store in zip(loads, stores):
        load.wait()
        store.start()
    for copy in stores:
        copy.wait()


def per_device(n, reps, queries, key_states, value_states, out_grad, doc_lengths):
    rows, key_width = key_states.shape
    kv_heads = key_width // HD
    width = rows * (queries.shape[1] // key_width)
    like = [jax.ShapeDtypeStruct(x.shape, x.dtype) for x in (queries, queries, key_states, key_states)]
    sems = pltpu.SemaphoreType.DMA((kv_heads, REACH))
    hbm = pl.BlockSpec(memory_space=pltpu.HBM)
    results = pl.pallas_call(
        functools.partial(kernel, n, reps),
        out_shape=like,
        in_specs=[hbm] * 5,
        out_specs=[hbm] * 4,
        scratch_shapes=[
            *(pltpu.VMEM(x.shape, x.dtype) for x in like),
            pltpu.SemaphoreType.DMA((kv_heads, 4)),
            pltpu.SMEM(doc_lengths.shape, jnp.int32),
            pltpu.VMEM(queries.shape, queries.dtype),
            pltpu.VMEM(out_grad.shape, out_grad.dtype),
            pltpu.VMEM((kv_heads, REACH + 1, rows, 2 * HD), jnp.bfloat16),
            pltpu.VMEM((kv_heads, REACH, rows, 2 * HD), jnp.bfloat16),
            pltpu.VMEM((kv_heads, REACH, rows, 2 * HD), jnp.bfloat16),
            pltpu.VMEM((REACH + 1, rows, width), jnp.float32),
            pltpu.VMEM((REACH + 1, rows, width), jnp.bfloat16),
            pltpu.SemaphoreType.DMA((3 + 2 * kv_heads,)),
            sems, sems, sems, sems,
        ],
        compiler_params=pltpu.CompilerParams(
            collective_id=0, has_side_effects=True, vmem_limit_bytes=63 * 1024 * 1024
        ),
    )(doc_lengths, queries, key_states, value_states, out_grad)
    return tuple(
        pl.pallas_call(
            flush,
            out_shape=like,
            in_specs=[hbm] * 4,
            out_specs=[hbm] * 4,
            scratch_shapes=[
                *(pltpu.VMEM(x.shape, x.dtype) for x in like),
                pltpu.SemaphoreType.DMA((2, 4)),
            ],
        )(*results)
    )


def solution(mesh):
    split = P(("ctx", "rep"), "tp")
    reps = mesh.shape["rep"]
    return jax.shard_map(
        functools.partial(per_device, mesh.shape["ctx"] * reps, reps),
        mesh=mesh,
        in_specs=(split, split, split, split, P()),
        out_specs=(split, split, split, split),
        check_vma=False,
    )
```
